128 devices in a mesh: panel: 4 (over x_lo, core), grp: 32 (over y, x_hi, z).
Axes of the slice: x: 4 (x_hi: 2, x_lo: 2; x = x_hi * 2 + x_lo), y: 4, z: 4, core: 2. Of those that a mesh axis runs over, the one named last changes fastest.
Arguments:
- b_blocks: bfloat16 [16384, 2048], P('grp', 'panel'), may hold values from -6 to 6
- w_store: bfloat16 [16384, 16384], P('grp', 'panel'), may hold values from -0.046875 to 0.046875
- owner: int32 [4], replicated, may hold values from 0 to 3, each once
- trials: bfloat16 [2048, 64], P(('panel', 'grp')), may hold values from -6 to 6
- eps_occ: float32 [128], replicated, may hold values from -3 to -0.5
- eps_virt: float32 [2048], replicated, may hold values from 0.5 to 3
- slab_first: int32 [1], replicated, may hold values from 0 to 127
Outputs:
- kernel_blocks: bfloat16 [2048, 16384], P(('panel', 'grp'))
- sigma: float32 [2048, 64], P(('panel', 'grp'))
The draws below stay inside these ranges and needn't reach their ends.
Inputs may be any that keep to these rules, and one draw needn't show every extreme that they name: owner names every panel index once.
All inputs are finite; a program needn't handle non-finite values.
Results may differ from the reference program's by a relative error of at most 0.007.
Values may be sent and summed in bfloat16 or wider, within the bound.
No kernel may reach another device: no remote copies, remote signals or barrier semaphores. Data moves between devices by JAX's collectives and lax.ppermute only.
A program may use at most 128 MiB of HBM per device.

```python
import math
import jax
import jax.numpy as jnp

NAUX = 16384
NV = 2048
NOCC = 128
NVEC = 64
OCC = 1
NT = 2048
N_PANEL = 4


def steps_of(rng, shape, pieces, smallest, largest):
    level = 1.0
    for dim, parts in pieces:
        draws = jax.random.uniform(jax.random.fold_in(jax.random.fold_in(rng, 6), dim), (parts,), jnp.float32, smallest / len(pieces), largest / len(pieces))
        level = level * jnp.repeat(jnp.exp(draws), shape[dim] // parts).reshape((-1,) + (1,) * (len(shape) - 1 - dim))
    return level


def centred(rng, dims, scale, reach, shards=(), held_as=jnp.bfloat16):
    loudness = steps_of(rng, dims, shards, -0.22, 0.18) if shards else 1.0
    entries = jax.random.normal(rng, dims, jnp.float32) * scale * loudness
    return jnp.minimum(jnp.maximum(entries, -reach), reach).astype(held_as)


def setup_inputs(seed: int = 0) -> dict:
    key_list = jax.random.split(jax.random.key(seed), 8)
    b_blocks = centred(key_list[0], (NAUX, NT), 1.0, 6.0, ((0, 32), (1, 4)))
    w_store = centred(key_list[1], (NAUX, NAUX), NAUX ** -0.5, 0.046875, ((0, 32), (1, 4)))
    owner = jax.random.permutation(key_list[2], N_PANEL).astype(jnp.int32)
    trials = centred(key_list[3], (NT, NVEC), 1.0, 6.0, ((0, 128),))
    eps_occ = jnp.clip(jax.random.uniform(key_list[4], (NOCC,), jnp.float32, -3.0, -0.5), -3.0, -0.5)
    eps_virt = jnp.clip(jax.random.uniform(key_list[5], (NV,), jnp.float32, 0.5, 3.0), 0.5, 3.0)
    slab_first = jax.random.randint(key_list[6], (1,), 0, NOCC - OCC + 1).astype(jnp.int32)
    return {"b_blocks": b_blocks, "w_store": w_store, "owner": owner, "trials": trials, "eps_occ": eps_occ, "eps_virt": eps_virt, "slab_first": slab_first}


def reference(b_blocks, w_store, owner, trials, eps_occ, eps_virt, slab_first):
    blocks = w_store.reshape(NAUX, N_PANEL, NAUX // N_PANEL)
    w_full = jnp.take(blocks, owner.astype(jnp.int32), axis=1).reshape(NAUX, NAUX)
    contracted = jnp.dot(w_full, b_blocks, preferred_element_type=jnp.float32)
    kernel = (2.0 * b_blocks.astype(jnp.float32) - contracted).astype(jnp.bfloat16)
    kernel_blocks = kernel.T
    projected = jnp.dot(b_blocks, trials, preferred_element_type=jnp.float32).astype(jnp.bfloat16)
    coupling = jnp.dot(kernel_blocks, projected, preferred_element_type=jnp.float32)
    index = jnp.arange(NT, dtype=jnp.int32)
    occupied = eps_occ[(slab_first[0] + index // NV).astype(jnp.int32)]
    virtual = eps_virt[(index % NV).astype(jnp.int32)]
    sigma = (virtual - occupied)[:, None] * trials.astype(jnp.float32) + coupling * (1.0 / math.sqrt(NAUX * NT))
    return (kernel_blocks, sigma)
```

```python
import math

import jax
import jax.numpy as jnp
from jax import lax
from jax.sharding import Mesh
from jax.sharding import PartitionSpec as P

NAUX = 16384
NV = 2048
NT = 2048
NVEC = 64

SIZES = {"xl": 2, "c": 2, "y": 4, "xh": 2, "z": 4}
AXES = tuple(SIZES)
GRP = ("y", "xh", "z")
PANEL = ("xl", "c")
PEERS = ("xl", "y", "xh", "z")


def move(value, axes, target):
    sizes = [SIZES[a] for a in axes]
    total = math.prod(sizes)
    pairs = []
    for source in range(total):
        rest, where = source, {}
        for axis, size in zip(reversed(axes), reversed(sizes)):
            rest, where[axis] = divmod(rest, size)
        there = target(where)
        if there is None:
            continue
        index = 0
        for axis, size in zip(axes, sizes):
            index = index * size + there[axis] % size
        pairs.append((source, index))
    return lax.ppermute(value, axes if len(axes) > 1 else axes[0], pairs)


def shift(value, axis, by):
    return move(value, (axis,), lambda w: {axis: w[axis] + by})


def along(value, by):
    return turn(value, by, 0)


def turn(value, by, x_core):
    def target(w):
        there = dict(w)
        if w["c"] == x_core:
            x = (2 * w["xh"] + w["xl"] + by) % 4
            there["xl"], there["xh"] = x % 2, x // 2
        else:
            there["z"] = w["z"] + by
        return there

    return move(value, ("xl", "c", "xh", "z"), target)


def keeps(w):
    return w["c"] == w["y"] % 2


def to_neighbour_plane(value, by):
    return move(
        value, ("c", "y"), lambda w: None if keeps(w) else {"c": 1 - w["c"], "y": w["y"] + by}
    )


def dot_tt(left, right):
    return lax.dot_general(
        left, right, (((1,), (1,)), ((), ())), preferred_element_type=jnp.float32
    )


def after(value, *others):
    return lax.optimization_barrier((value,) + others)[0]


def on_device(b_blocks, w_store, owner, trials, eps_occ, eps_virt, slab_first):
    xl, c, y = lax.axis_index("xl"), lax.axis_index("c"), lax.axis_index("y")
    xh, z = lax.axis_index("xh"), lax.axis_index("z")
    parity = lax.rem(y, 2)
    keeper = c == parity
    low = xl == 0
    first_core = c == 0

    bt = b_blocks.T.reshape(32, 2, 8, 512).transpose(1, 0, 2, 3).reshape(512, 512)
    from_below, from_above = shift(bt, "y", 1), shift(bt, "y", -1)
    from_across = shift(bt, "y", 2)

    def rows_of(place):
        plane = jnp.sum(jnp.where(owner == place, jnp.arange(4, dtype=jnp.int32), 0))
        off = lax.rem(y - plane + 4, 4)
        return jnp.where(
            off < 2,
            jnp.where(off == 0, bt, from_below),
            jnp.where(off == 2, from_across, from_above),
        )

    mine = rows_of(2 * xl + parity)
    theirs = rows_of(2 * (1 - xl) + parity)
    pair = jnp.stack([mine, theirs])

    p1, p2, p3 = along(pair, -1), along(pair, 2), along(pair, 1)

    w_late = after(w_store, pair)

    def column_blocks(rows):
        blocks = []
        for far in range(2):
            for step in range(4):
                group = jnp.where(far == 0, xh, 1 - xh) * 4 + lax.rem(z + step, 4)
                blocks.append(lax.dynamic_slice(w_late, (rows, group * 512), (256, 512)))
        return jnp.stack(blocks)

    w_lo, w_hi = column_blocks(0), column_blocks(256)
    below, above = to_neighbour_plane(w_lo, 1), to_neighbour_plane(w_hi, -1)
    swap_lo = shift(jnp.where(keeper, w_lo, below), "c", 1)
    swap_hi = shift(jnp.where(keeper, w_hi, above), "c", 1)
    w_all = jnp.stack(
        [
            jnp.where(keeper, w_lo, swap_lo),
            jnp.where(keeper, w_hi, swap_hi),
            jnp.where(keeper, swap_lo, below),
            jnp.where(keeper, swap_hi, above),
        ],
        axis=1,
    ).reshape(8, 1024, 512)

    def pick(core0, core1):
        return jnp.where(first_core, core0, core1)

    to_sides = jnp.stack([pick(mine, theirs), p1[1], pick(p2[0], p2[1]), p3[1]])
    to_across = jnp.stack([mine, pick(p1[1], p1[0]), p2[0], pick(p3[1], p3[0])])

    copies = jnp.broadcast_to(after(trials, p1, p2, p3), (32,) + trials.shape)
    trial_rows = lax.all_to_all(copies, GRP, split_axis=0, concat_axis=0).reshape(512, NVEC)
    terms = jnp.dot(b_blocks, trial_rows, preferred_element_type=jnp.float32)
    terms = terms + shift(terms, "c", 1)
    proj = (terms + shift(terms, "xl", 1)).astype(jnp.bfloat16)
    proj_rows = jnp.concatenate(
        [proj, shift(proj[:256], "y", 1), shift(proj[256:], "y", -1)], axis=0
    )

    def block(g, u):
        index = []
        for x_off, z_off in ((u, g), (g, u)):
            far = {0: 0, 2: 1, 1: 1 - low.astype(jnp.int32), 3: low.astype(jnp.int32)}[x_off]
            index.append(far * 4 + z_off)
        return lax.dynamic_index_in_dim(w_all, pick(*index), 0, keepdims=False)

    def finish(half):
        rows = slice(half * 256, half * 256 + 256)
        sides, across = to_sides[:, rows], to_across[:, rows]
        pieces = [across, turn(sides, -1, 1), turn(across, 2, 1), turn(sides, 1, 1)]
        sums = {}
        for g in (0, 1, 3, 2):
            for u in range(4):
                term = dot_tt(pieces[g][u], block(g, u))
                key = (g % 2, u % 2)
                sums[key] = sums[key] + term if key in sums else term
        same = sums[0, 0] + pick(sums[1, 0], sums[0, 1])
        opposite = sums[1, 1] + pick(sums[0, 1], sums[1, 0])
        twice = 2.0 * bt[rows].astype(jnp.float32)
        same = jnp.concatenate([twice - same[:, :512], -same[:, 512:]], axis=1)

        def message(part):
            rounded = part.astype(jnp.bfloat16)
            coupled = jnp.dot(rounded, proj_rows, preferred_element_type=jnp.float32)
            high = coupled.astype(jnp.bfloat16)
            rest = (coupled - high.astype(jnp.float32)).astype(jnp.bfloat16)
            return jnp.concatenate([rounded, high, rest], axis=1)

        m_same, m_opp = message(same), message(-opposite)
        out = jnp.stack([jnp.where(low, m_same, m_opp), jnp.where(low, m_opp, m_same)])
        got = lax.all_to_all(out.reshape(64, 8, 1152), PEERS, split_axis=0, concat_axis=0)
        got = got.astype(jnp.float32).reshape(2, 4, 8, 8, 1152).sum(axis=0)
        first = jnp.roll(got[..., 512:768], -1, axis=0)
        second = jnp.roll(got[..., 768:1024], 1, axis=0)
        kernel = got[..., :512] + jnp.concatenate([first, second], axis=-1)
        kernel = kernel.astype(jnp.bfloat16).transpose(2, 0, 1, 3).reshape(8, NAUX)
        return kernel, jnp.sum(got[..., 1024:1088] + got[..., 1088:], axis=(0, 1))

    halves = [finish(half) for half in range(2)]
    kernel_rows = jnp.concatenate([k for k, _ in halves], axis=0)
    coupling = jnp.concatenate([v for _, v in halves], axis=0)

    rows_here = 16
    first_row = ((xl * 2 + c) * 32 + y * 8 + xh * 4 + z) * rows_here
    occ_index = slab_first[0] + first_row // NV
    positions = jnp.arange(eps_occ.shape[0], dtype=jnp.int32)
    occupied = jnp.sum(jnp.where(positions == occ_index, eps_occ, 0.0))
    virtual = lax.dynamic_slice_in_dim(eps_virt, first_row % NV, rows_here, 0)
    diagonal = (virtual - occupied)[:, None]
    sigma = diagonal * trials.astype(jnp.float32) + coupling * (1.0 / math.sqrt(NAUX * NT))
    return (kernel_rows, sigma)


def solution(mesh):
    fine = Mesh(mesh.devices.reshape(tuple(SIZES.values())), AXES)
    in_specs = (P(GRP, PANEL), P(GRP, PANEL), P(), P(PANEL + GRP, None), P(), P(), P())
    out_specs = (P(PANEL + GRP, None), P(PANEL + GRP, None))
    return jax.shard_map(
        on_device, mesh=fine, in_specs=in_specs, out_specs=out_specs, check_vma=False
    )
```

```python
import math

import jax
import jax.numpy as jnp
from jax import lax
from jax.experimental import pallas as pl
from jax.experimental.pallas import tpu as pltpu
from jax.sharding import Mesh
from jax.sharding import PartitionSpec as P

NAUX = 16384
NV = 2048
NT = 2048
NVEC = 64
PARTS = (8, 8)

SIZES = {"xl": 2, "c": 2, "y": 4, "xh": 2, "z": 4}
AXES = tuple(SIZES)
GRP = ("y", "xh", "z")
PANEL = ("xl", "c")
PEERS = ("xl", "y", "xh", "z")


def move(value, axes, target):
    sizes = [SIZES[a] for a in axes]
    total = math.prod(sizes)
    pairs = []
    for source in range(total):
        rest, where = source, {}
        for axis, size in zip(reversed(axes), reversed(sizes)):
            rest, where[axis] = divmod(rest, size)
        there = target(where)
        if there is None:
            continue
        index = 0
        for axis, size in zip(axes, sizes):
            index = index * size + there[axis] % size
        pairs.append((source, index))
    return lax.ppermute(value, axes if len(axes) > 1 else axes[0], pairs)


def shift(value, axis, by):
    return move(value, (axis,), lambda w: {axis: w[axis] + by})


def along(value, by):
    return turn(value, by, 0)


def turn(value, by, x_core):
    def target(w):
        there = dict(w)
        if w["c"] == x_core:
            x = (2 * w["xh"] + w["xl"] + by) % 4
            there["xl"], there["xh"] = x % 2, x // 2
        else:
            there["z"] = w["z"] + by
        return there

    return move(value, ("xl", "c", "xh", "z"), target)


def keeps(w):
    return w["c"] == w["y"] % 2


def to_neighbour_plane(value, by):
    return move(
        value, ("c", "y"), lambda w: None if keeps(w) else {"c": 1 - w["c"], "y": w["y"] + by}
    )


MESSAGE = 1024 + 2 * NVEC


def finish_kernel(table, g0, g1, g2, g3, w_all, bt, proj, out):
    count = out.shape[1]
    pieces = (g0, g1, g2, g3)
    first_core = table[16] == 1

    def on_block(block, coupled):
        rows = pl.multiple_of(block * 256, 256)
        sums = {}
        for g in range(4):
            for u in range(4):
                column = pl.multiple_of(table[4 * g + u] * 512, 512)
                term = lax.dot_general(
                    pieces[g][u],
                    w_all[pl.ds(rows, 256), pl.ds(column, 512)],
                    (((1,), (1,)), ((), ())),
                    preferred_element_type=jnp.float32,
                )
                key = (g % 2, u % 2)
                sums[key] = sums[key] + term if key in sums else term
        mixed = (sums[0, 1], sums[1, 0])
        same = sums[0, 0] + jnp.where(first_core, mixed[1], mixed[0])
        opposite = sums[1, 1] + jnp.where(first_core, mixed[0], mixed[1])
        own = jnp.where(block < 2, 2.0, 0.0)
        same = own * bt[:, pl.ds(pl.multiple_of(lax.rem(rows, 512), 256), 256)].astype(jnp.float32) - same
        added = []
        for slot, part in enumerate((same, -opposite)):
            rounded = part.astype(jnp.bfloat16)
            out[table[17 + slot], :, pl.ds(rows, 256)] = rounded
            added.append(
                coupled[slot]
                + lax.dot_general(
                    rounded,
                    proj[:, pl.ds(rows, 256)],
                    (((1,), (1,)), ((), ())),
                    preferred_element_type=jnp.float32,
                )
            )
        return tuple(added)

    coupled = lax.fori_loop(0, 4, on_block, (jnp.zeros((count, 2 * NVEC), jnp.float32),) * 2)
    high_lanes = lax.broadcasted_iota(jnp.int32, (count, 2 * NVEC), 1) < NVEC
    for slot in range(2):
        high = coupled[slot].astype(jnp.bfloat16).astype(jnp.float32)
        both = jnp.where(high_lanes, high, coupled[slot] - high)
        out[table[17 + slot], :, 1024:] = both.astype(jnp.bfloat16)


def finish_part(table, pieces, w_all, bt, proj):
    count = bt.shape[0]
    in_vmem = pl.BlockSpec(memory_space=pltpu.VMEM)
    return pl.pallas_call(
        finish_kernel,
        out_shape=jax.ShapeDtypeStruct((2, count, MESSAGE), jnp.bfloat16),
        in_specs=[pl.BlockSpec(memory_space=pltpu.SMEM)] + [in_vmem] * 7,
        out_specs=in_vmem,
        compiler_params=pltpu.CompilerParams(vmem_limit_bytes=40 * 2**20),
        cost_estimate=pl.CostEstimate(
            flops=2 * 2 * count * 1024 * 4096, bytes_accessed=14 * 2**20, transcendentals=0
        ),
    )(table, *pieces, w_all, bt, proj)


def after(value, seen):
    ready = jnp.abs(seen[0, 0]) < 1e30
    return jnp.where(ready, value, jnp.zeros_like(value))


def on_device(b_blocks, w_store, owner, trials, eps_occ, eps_virt, slab_first):
    xl, c, y = lax.axis_index("xl"), lax.axis_index("c"), lax.axis_index("y")
    xh, z = lax.axis_index("xh"), lax.axis_index("z")
    parity = lax.rem(y, 2)
    keeper = c == parity
    low = xl == 0
    first_core = c == 0

    starts = [sum(PARTS[:k]) for k in range(len(PARTS))]
    bt = b_blocks.T.reshape(32, 16, 512)
    bt = jnp.concatenate(
        [bt[:, at : at + n].reshape(32 * n, 512) for at, n in zip(starts, PARTS)], axis=0
    )
    from_below, from_above = shift(bt, "y", 1), shift(bt, "y", -1)
    from_across = shift(bt, "y", 2)

    def rows_of(place):
        plane = jnp.sum(jnp.where(owner == place, jnp.arange(4, dtype=jnp.int32), 0))
        off = lax.rem(y - plane + 4, 4)
        return jnp.where(
            off < 2,
            jnp.where(off == 0, bt, from_below),
            jnp.where(off == 2, from_across, from_above),
        )

    mine = rows_of(2 * xl + parity)
    theirs = rows_of(2 * (1 - xl) + parity)
    copies = jnp.broadcast_to(after(trials, shift(bt[:16], "c", 1)), (8,) + trials.shape)
    plane_trials = lax.all_to_all(copies, ("xh", "z"), split_axis=0, concat_axis=0)
    copies = jnp.broadcast_to(plane_trials, (4, 8) + trials.shape)
    trial_rows = lax.all_to_all(copies, "y", split_axis=0, concat_axis=0).reshape(512, NVEC)
    terms = lax.dot_general(
        trial_rows, b_blocks, (((0,), (1,)), ((), ())), preferred_element_type=jnp.float32
    )
    terms = terms + shift(terms, "c", 1)

    load = jnp.concatenate([mine, theirs, terms.astype(jnp.bfloat16)], axis=0)
    p1, p2, p3 = along(load, -1), along(load, 2), along(load, 1)

    seen = shift(load[:16], "c", 1)
    w_lo, w_hi = after(w_store[:256], seen), after(w_store[256:], seen)
    below, above = to_neighbour_plane(w_lo, 1), to_neighbour_plane(w_hi, -1)
    def pick(core0, core1):
        return jnp.where(first_core, core0, core1)

    def gathered(rows):
        own = mine[rows]
        q1, q2, q3 = ((p[:512][rows], p[512:1024][rows]) for p in (p1, p2, p3))
        to_sides = jnp.stack([pick(own, theirs[rows]), q1[1], pick(q2[0], q2[1]), q3[1]])
        to_across = jnp.stack([own, pick(q1[1], q1[0]), q2[0], pick(q3[1], q3[0])])
        return [to_across, turn(to_sides, -1, 1), turn(to_across, 2, 1), turn(to_sides, 1, 1)]

    starts_at = [32 * at for at in starts]
    gathered_parts = [
        gathered(slice(at, at + 32 * n)) for at, n in zip(starts_at, PARTS)
    ]
    seen = shift(gathered_parts[0][0][0, :16], "c", 1)
    swap_lo = shift(after(jnp.where(keeper, w_lo, below), seen), "c", 1)
    swap_hi = shift(after(jnp.where(keeper, w_hi, above), seen), "c", 1)
    w_all = jnp.concatenate(
        [
            jnp.where(keeper, w_lo, swap_lo),
            jnp.where(keeper, w_hi, swap_hi),
            jnp.where(keeper, swap_lo, below),
            jnp.where(keeper, swap_hi, above),
        ],
        axis=0,
    )

    from_pair = after(jnp.where(low, p1[1024:], p3[1024:]), seen)
    from_pair = pick(from_pair, shift(from_pair, "c", 1))
    proj = (terms + from_pair.astype(jnp.float32)).astype(jnp.bfloat16)
    proj = jnp.concatenate([proj, proj], axis=0)
    proj_rows = jnp.concatenate(
        [proj, shift(proj[:, :256], "y", 1), shift(proj[:, 256:], "y", -1)], axis=1
    )

    columns = []
    for g in range(4):
        for u in range(4):
            options = []
            for x_off, z_off in ((u, g), (g, u)):
                far = (0, 1 - low.astype(jnp.int32), 1, low.astype(jnp.int32))[x_off]
                options.append(jnp.where(far == 0, xh, 1 - xh) * 4 + lax.rem(z + z_off, 4))
            columns.append(pick(*options))
    table = jnp.stack(columns + [1 - c, xl, 1 - xl])

    def finish(pieces, at, n):
        out = finish_part(table, pieces, w_all, bt[32 * at : 32 * (at + n)], proj_rows)
        got = lax.all_to_all(out.reshape(64, n, MESSAGE), PEERS, split_axis=0, concat_axis=0)
        got = got.astype(jnp.float32).reshape(2, 4, 8, n, MESSAGE).sum(axis=0)
        first = jnp.roll(got[..., 512:768], -1, axis=0)
        second = jnp.roll(got[..., 768:1024], 1, axis=0)
        kernel = got[..., :512] + jnp.concatenate([first, second], axis=-1)
        kernel = kernel.astype(jnp.bfloat16).transpose(2, 0, 1, 3).reshape(n, NAUX)
        return kernel, jnp.sum(got[..., 1024:1088] + got[..., 1088:], axis=(0, 1))

    parts = [finish(*part) for part in zip(gathered_parts, starts, PARTS)]
    kernel_rows = jnp.concatenate([k for k, _ in parts], axis=0)
    coupling = jnp.concatenate([v for _, v in parts], axis=0)

    rows_here = 16
    first_row = ((xl * 2 + c) * 32 + y * 8 + xh * 4 + z) * rows_here
    occ_index = slab_first[0] + first_row // NV
    positions = jnp.arange(eps_occ.shape[0], dtype=jnp.int32)
    occupied = jnp.sum(jnp.where(positions == occ_index, eps_occ, 0.0))
    virtual = lax.dynamic_slice_in_dim(eps_virt, first_row % NV, rows_here, 0)
    diagonal = (virtual - occupied)[:, None]
    sigma = diagonal * trials.astype(jnp.float32) + coupling * (1.0 / math.sqrt(NAUX * NT))
    return (kernel_rows, sigma)


def solution(mesh):
    fine = Mesh(mesh.devices.reshape(tuple(SIZES.values())), AXES)
    in_specs = (P(GRP, PANEL), P(GRP, PANEL), P(), P(PANEL + GRP, None), P(), P(), P())
    out_specs = (P(PANEL + GRP, None), P(PANEL + GRP, None))
    return jax.shard_map(
        on_device, mesh=fine, in_specs=in_specs, out_specs=out_specs, check_vma=False
    )
```

```python
import math

import jax
import jax.numpy as jnp
from jax import lax
from jax.experimental import pallas as pl
from jax.experimental.pallas import tpu as pltpu
from jax.sharding import Mesh
from jax.sharding import PartitionSpec as P

NAUX = 16384
NV = 2048
NT = 2048
NVEC = 64
PARTS = (8, 8)

SIZES = {"xl": 2, "c": 2, "y": 4, "xh": 2, "z": 4}
AXES = tuple(SIZES)
GRP = ("y", "xh", "z")
PANEL = ("xl", "c")
PEERS = ("xl", "y", "xh", "z")


def move(value, axes, target):
    sizes = [SIZES[a] for a in axes]
    total = math.prod(sizes)
    pairs = []
    for source in range(total):
        rest, where = source, {}
        for axis, size in zip(reversed(axes), reversed(sizes)):
            rest, where[axis] = divmod(rest, size)
        there = target(where)
        if there is None:
            continue
        index = 0
        for axis, size in zip(axes, sizes):
            index = index * size + there[axis] % size
        pairs.append((source, index))
    return lax.ppermute(value, axes if len(axes) > 1 else axes[0], pairs)


def shift(value, axis, by):
    return move(value, (axis,), lambda w: {axis: w[axis] + by})


def along(value, by):
    return turn(value, by, 0)


def turn(value, by, x_core):
    def target(w):
        there = dict(w)
        if w["c"] == x_core:
            x = (2 * w["xh"] + w["xl"] + by) % 4
            there["xl"], there["xh"] = x % 2, x // 2
        else:
            there["z"] = w["z"] + by
        return there

    return move(value, ("xl", "c", "xh", "z"), target)


def keeps(w):
    return w["c"] == w["y"] % 2


def to_neighbour_plane(value, by):
    return move(
        value, ("c", "y"), lambda w: None if keeps(w) else {"c": 1 - w["c"], "y": w["y"] + by}
    )


MESSAGE = 1024 + 2 * NVEC


def finish_kernel(table, g0, g1, g2, g3, w_all, bt, proj, out):
    count = out.shape[1]
    pieces = (g0, g1, g2, g3)
    first_core = table[16] == 1

    def on_block(block, coupled):
        rows = pl.multiple_of(block * 256, 256)
        sums = {}
        for g in range(4):
            for u in range(4):
                column = pl.multiple_of(table[4 * g + u] * 512, 512)
                term = lax.dot_general(
                    pieces[g][u],
                    w_all[pl.ds(rows, 256), pl.ds(column, 512)],
                    (((1,), (1,)), ((), ())),
                    preferred_element_type=jnp.float32,
                )
                key = (g % 2, u % 2)
                sums[key] = sums[key] + term if key in sums else term
        mixed = (sums[0, 1], sums[1, 0])
        same = sums[0, 0] + jnp.where(first_core, mixed[1], mixed[0])
        opposite = sums[1, 1] + jnp.where(first_core, mixed[0], mixed[1])
        own = jnp.where(block < 2, 2.0, 0.0)
        same = own * bt[:, pl.ds(pl.multiple_of(lax.rem(rows, 512), 256), 256)].astype(jnp.float32) - same
        added = []
        for slot, part in enumerate((same, -opposite)):
            rounded = part.astype(jnp.bfloat16)
            out[table[17 + slot], :, pl.ds(rows, 256)] = rounded
            added.append(
                coupled[slot]
                + lax.dot_general(
                    rounded,
                    proj[:, pl.ds(rows, 256)],
                    (((1,), (1,)), ((), ())),
                    preferred_element_type=jnp.float32,
                )
            )
        return tuple(added)

    coupled = lax.fori_loop(0, 4, on_block, (jnp.zeros((count, 2 * NVEC), jnp.float32),) * 2)
    high_lanes = lax.broadcasted_iota(jnp.int32, (count, 2 * NVEC), 1) < NVEC
    for slot in range(2):
        high = coupled[slot].astype(jnp.bfloat16).astype(jnp.float32)
        both = jnp.where(high_lanes, high, coupled[slot] - high)
        out[table[17 + slot], :, 1024:] = both.astype(jnp.bfloat16)


def finish_part(table, pieces, w_all, bt, proj):
    count = bt.shape[0]
    in_vmem = pl.BlockSpec(memory_space=pltpu.VMEM)
    return pl.pallas_call(
        finish_kernel,
        out_shape=jax.ShapeDtypeStruct((2, count, MESSAGE), jnp.bfloat16),
        in_specs=[pl.BlockSpec(memory_space=pltpu.SMEM)] + [in_vmem] * 7,
        out_specs=in_vmem,
        compiler_params=pltpu.CompilerParams(vmem_limit_bytes=40 * 2**20),
        cost_estimate=pl.CostEstimate(
            flops=2 * 2 * count * 1024 * 4096, bytes_accessed=14 * 2**20, transcendentals=0
        ),
    )(table, *pieces, w_all, bt, proj)


def after(value, seen):
    ready = jnp.abs(seen[0, 0]) < 1e30
    return jnp.where(ready, value, jnp.zeros_like(value))


def on_device(b_blocks, w_store, owner, trials, eps_occ, eps_virt, slab_first):
    xl, c, y = lax.axis_index("xl"), lax.axis_index("c"), lax.axis_index("y")
    xh, z = lax.axis_index("xh"), lax.axis_index("z")
    parity = lax.rem(y, 2)
    keeper = c == parity
    low = xl == 0
    first_core = c == 0

    starts = [sum(PARTS[:k]) for k in range(len(PARTS))]
    bt = b_blocks.T.reshape(32, 16, 512)
    bt = jnp.concatenate(
        [bt[:, at : at + n].reshape(32 * n, 512) for at, n in zip(starts, PARTS)], axis=0
    )
    from_below, from_above = shift(bt, "y", 1), shift(bt, "y", -1)
    from_across = shift(bt, "y", 2)

    def rows_of(place):
        plane = jnp.sum(jnp.where(owner == place, jnp.arange(4, dtype=jnp.int32), 0))
        off = lax.rem(y - plane + 4, 4)
        return jnp.where(
            off < 2,
            jnp.where(off == 0, bt, from_below),
            jnp.where(off == 2, from_across, from_above),
        )

    mine = rows_of(2 * xl + parity)
    theirs = rows_of(2 * (1 - xl) + parity)
    copies = jnp.broadcast_to(after(trials, shift(bt[:16], "c", 1)), (8,) + trials.shape)
    plane_trials = lax.all_to_all(copies, ("xh", "z"), split_axis=0, concat_axis=0)
    copies = jnp.broadcast_to(plane_trials, (4, 8) + trials.shape)
    trial_rows = lax.all_to_all(copies, "y", split_axis=0, concat_axis=0).reshape(512, NVEC)
    terms = lax.dot_general(
        trial_rows, b_blocks, (((0,), (1,)), ((), ())), preferred_element_type=jnp.float32
    )
    terms = terms + shift(terms, "c", 1)

    load = jnp.concatenate([mine, theirs, terms.astype(jnp.bfloat16)], axis=0)
    p1, p2, p3 = along(load, -1), along(load, 2), along(load, 1)

    seen = shift(load[:16], "c", 1)
    w_lo, w_hi = after(w_store[:256], seen), after(w_store[256:], seen)
    below, above = to_neighbour_plane(w_lo, 1), to_neighbour_plane(w_hi, -1)
    def pick(core0, core1):
        return jnp.where(first_core, core0, core1)

    def gathered(rows):
        own = mine[rows]
        q1, q2, q3 = ((p[:512][rows], p[512:1024][rows]) for p in (p1, p2, p3))
        to_sides = jnp.stack([pick(own, theirs[rows]), q1[1], pick(q2[0], q2[1]), q3[1]])
        to_across = jnp.stack([own, pick(q1[1], q1[0]), q2[0], pick(q3[1], q3[0])])
        return [to_across, turn(to_sides, -1, 1), turn(to_across, 2, 1), turn(to_sides, 1, 1)]

    starts_at = [32 * at for at in starts]
    gathered_parts = [
        gathered(slice(at, at + 32 * n)) for at, n in zip(starts_at, PARTS)
    ]
    swap_lo = shift(jnp.where(keeper, w_lo, below), "c", 1)
    swap_hi = shift(jnp.where(keeper, w_hi, above), "c", 1)
    w_all = jnp.concatenate(
        [
            jnp.where(keeper, w_lo, swap_lo),
            jnp.where(keeper, w_hi, swap_hi),
            jnp.where(keeper, swap_lo, below),
            jnp.where(keeper, swap_hi, above),
        ],
        axis=0,
    )

    from_pair = jnp.where(low, p1[1024:], p3[1024:])
    from_pair = pick(from_pair, shift(from_pair, "c", 1))
    proj = (terms + from_pair.astype(jnp.float32)).astype(jnp.bfloat16)
    proj = jnp.concatenate([proj, proj], axis=0)
    proj_rows = jnp.concatenate(
        [proj, shift(proj[:, :256], "y", 1), shift(proj[:, 256:], "y", -1)], axis=1
    )

    columns = []
    for g in range(4):
        for u in range(4):
            options = []
            for x_off, z_off in ((u, g), (g, u)):
                far = (0, 1 - low.astype(jnp.int32), 1, low.astype(jnp.int32))[x_off]
                options.append(jnp.where(far == 0, xh, 1 - xh) * 4 + lax.rem(z + z_off, 4))
            columns.append(pick(*options))
    table = jnp.stack(columns + [1 - c, xl, 1 - xl])

    def finish(pieces, at, n):
        out = finish_part(table, pieces, w_all, bt[32 * at : 32 * (at + n)], proj_rows)
        got = lax.all_to_all(out.reshape(64, n, MESSAGE), PEERS, split_axis=0, concat_axis=0)
        got = got.astype(jnp.float32).reshape(2, 4, 8, n, MESSAGE).sum(axis=0)
        first = jnp.roll(got[..., 512:768], -1, axis=0)
        second = jnp.roll(got[..., 768:1024], 1, axis=0)
        kernel = got[..., :512] + jnp.concatenate([first, second], axis=-1)
        kernel = kernel.astype(jnp.bfloat16).transpose(2, 0, 1, 3).reshape(n, NAUX)
        return kernel, jnp.sum(got[..., 1024:1088] + got[..., 1088:], axis=(0, 1))

    parts = [finish(*part) for part in zip(gathered_parts, starts, PARTS)]
    kernel_rows = jnp.concatenate([k for k, _ in parts], axis=0)
    coupling = jnp.concatenate([v for _, v in parts], axis=0)

    rows_here = 16
    first_row = ((xl * 2 + c) * 32 + y * 8 + xh * 4 + z) * rows_here
    occ_index = slab_first[0] + first_row // NV
    positions = jnp.arange(eps_occ.shape[0], dtype=jnp.int32)
    occupied = jnp.sum(jnp.where(positions == occ_index, eps_occ, 0.0))
    virtual = lax.dynamic_slice_in_dim(eps_virt, first_row % NV, rows_here, 0)
    diagonal = (virtual - occupied)[:, None]
    sigma = diagonal * trials.astype(jnp.float32) + coupling * (1.0 / math.sqrt(NAUX * NT))
    return (kernel_rows, sigma)


def solution(mesh):
    fine = Mesh(mesh.devices.reshape(tuple(SIZES.values())), AXES)
    in_specs = (P(GRP, PANEL), P(GRP, PANEL), P(), P(PANEL + GRP, None), P(), P(), P())
    out_specs = (P(PANEL + GRP, None), P(PANEL + GRP, None))
    return jax.shard_map(
        on_device, mesh=fine, in_specs=in_specs, out_specs=out_specs, check_vma=False
    )
```

```python
import math

import jax
import jax.numpy as jnp
from jax import lax
from jax.experimental import pallas as pl
from jax.experimental.pallas import tpu as pltpu
from jax.sharding import Mesh
from jax.sharding import PartitionSpec as P

NAUX = 16384
NV = 2048
NT = 2048
NVEC = 64
PARTS = (8, 8)

SIZES = {"xl": 2, "c": 2, "y": 4, "xh": 2, "z": 4}
AXES = tuple(SIZES)
GRP = ("y", "xh", "z")
PANEL = ("xl", "c")
PEERS = ("xl", "y", "xh", "z")


def move(value, axes, target):
    sizes = [SIZES[a] for a in axes]
    total = math.prod(sizes)
    pairs = []
    for source in range(total):
        rest, where = source, {}
        for axis, size in zip(reversed(axes), reversed(sizes)):
            rest, where[axis] = divmod(rest, size)
        there = target(where)
        if there is None:
            continue
        index = 0
        for axis, size in zip(axes, sizes):
            index = index * size + there[axis] % size
        pairs.append((source, index))
    return lax.ppermute(value, axes if len(axes) > 1 else axes[0], pairs)


def shift(value, axis, by):
    return move(value, (axis,), lambda w: {axis: w[axis] + by})


def along(value, by):
    return turn(value, by, 0)


def turn(value, by, x_core):
    def target(w):
        there = dict(w)
        if w["c"] == x_core:
            x = (2 * w["xh"] + w["xl"] + by) % 4
            there["xl"], there["xh"] = x % 2, x // 2
        else:
            there["z"] = w["z"] + by
        return there

    return move(value, ("xl", "c", "xh", "z"), target)


def keeps(w):
    return w["c"] == w["y"] % 2


def to_neighbour_plane(value, by):
    return move(
        value, ("c", "y"), lambda w: None if keeps(w) else {"c": 1 - w["c"], "y": w["y"] + by}
    )


MESSAGE = 1024 + 2 * NVEC


def finish_kernel(table, g0, g1, g2, g3, w_all, bt, proj, out):
    count = out.shape[1]
    pieces = (g0, g1, g2, g3)
    first_core = table[16] == 1

    def on_block(block, coupled):
        rows = pl.multiple_of(block * 512, 512)
        sums = {}
        for g in range(4):
            for u in range(4):
                column = pl.multiple_of(table[4 * g + u] * 512, 512)
                term = lax.dot_general(
                    pieces[g][u],
                    w_all[pl.ds(rows, 512), pl.ds(column, 512)],
                    (((1,), (1,)), ((), ())),
                    preferred_element_type=jnp.float32,
                )
                key = (g % 2, u % 2)
                sums[key] = sums[key] + term if key in sums else term
        mixed = (sums[0, 1], sums[1, 0])
        same = sums[0, 0] + jnp.where(first_core, mixed[1], mixed[0])
        opposite = sums[1, 1] + jnp.where(first_core, mixed[0], mixed[1])
        own = jnp.where(block < 1, 2.0, 0.0)
        same = own * bt[...].astype(jnp.float32) - same
        added = []
        for slot, part in enumerate((same, -opposite)):
            rounded = part.astype(jnp.bfloat16)
            out[table[17 + slot], :, pl.ds(rows, 512)] = rounded
            added.append(
                coupled[slot]
                + lax.dot_general(
                    rounded,
                    proj[:, pl.ds(rows, 512)],
                    (((1,), (1,)), ((), ())),
                    preferred_element_type=jnp.float32,
                )
            )
        return tuple(added)

    coupled = lax.fori_loop(0, 2, on_block, (jnp.zeros((count, 2 * NVEC), jnp.float32),) * 2)
    high_lanes = lax.broadcasted_iota(jnp.int32, (count, 2 * NVEC), 1) < NVEC
    for slot in range(2):
        high = coupled[slot].astype(jnp.bfloat16).astype(jnp.float32)
        both = jnp.where(high_lanes, high, coupled[slot] - high)
        out[table[17 + slot], :, 1024:] = both.astype(jnp.bfloat16)


def finish_part(table, pieces, w_all, bt, proj):
    count = bt.shape[0]
    in_vmem = pl.BlockSpec(memory_space=pltpu.VMEM)
    return pl.pallas_call(
        finish_kernel,
        out_shape=jax.ShapeDtypeStruct((2, count, MESSAGE), jnp.bfloat16),
        in_specs=[pl.BlockSpec(memory_space=pltpu.SMEM)] + [in_vmem] * 7,
        out_specs=in_vmem,
        compiler_params=pltpu.CompilerParams(vmem_limit_bytes=40 * 2**20),
        cost_estimate=pl.CostEstimate(
            flops=2 * 2 * count * 1024 * 4096, bytes_accessed=14 * 2**20, transcendentals=0
        ),
    )(table, *pieces, w_all, bt, proj)


def after(value, seen):
    ready = jnp.abs(seen[0, 0]) < 1e30
    return jnp.where(ready, value, jnp.zeros_like(value))


def on_device(b_blocks, w_store, owner, trials, eps_occ, eps_virt, slab_first):
    xl, c, y = lax.axis_index("xl"), lax.axis_index("c"), lax.axis_index("y")
    xh, z = lax.axis_index("xh"), lax.axis_index("z")
    parity = lax.rem(y, 2)
    keeper = c == parity
    low = xl == 0
    first_core = c == 0

    starts = [sum(PARTS[:k]) for k in range(len(PARTS))]
    bt = b_blocks.T.reshape(32, 16, 512)
    bt = jnp.concatenate(
        [bt[:, at : at + n].reshape(32 * n, 512) for at, n in zip(starts, PARTS)], axis=0
    )
    from_below, from_above = shift(bt, "y", 1), shift(bt, "y", -1)
    from_across = shift(bt, "y", 2)

    def rows_of(place):
        plane = jnp.sum(jnp.where(owner == place, jnp.arange(4, dtype=jnp.int32), 0))
        off = lax.rem(y - plane + 4, 4)
        return jnp.where(
            off < 2,
            jnp.where(off == 0, bt, from_below),
            jnp.where(off == 2, from_across, from_above),
        )

    mine = rows_of(2 * xl + parity)
    theirs = rows_of(2 * (1 - xl) + parity)
    copies = jnp.broadcast_to(after(trials, shift(bt[:16], "c", 1)), (8,) + trials.shape)
    plane_trials = lax.all_to_all(copies, ("xh", "z"), split_axis=0, concat_axis=0)
    copies = jnp.broadcast_to(plane_trials, (4, 8) + trials.shape)
    trial_rows = lax.all_to_all(copies, "y", split_axis=0, concat_axis=0).reshape(512, NVEC)
    terms = lax.dot_general(
        trial_rows, b_blocks, (((0,), (1,)), ((), ())), preferred_element_type=jnp.float32
    )
    terms = terms + shift(terms, "c", 1)

    load = jnp.concatenate([mine, theirs, terms.astype(jnp.bfloat16)], axis=0)
    p1, p2, p3 = along(load, -1), along(load, 2), along(load, 1)

    seen = shift(load[:16], "c", 1)
    w_lo, w_hi = after(w_store[:256], seen), after(w_store[256:], seen)
    below, above = to_neighbour_plane(w_lo, 1), to_neighbour_plane(w_hi, -1)
    def pick(core0, core1):
        return jnp.where(first_core, core0, core1)

    def gathered(rows):
        own = mine[rows]
        q1, q2, q3 = ((p[:512][rows], p[512:1024][rows]) for p in (p1, p2, p3))
        to_sides = jnp.stack([pick(own, theirs[rows]), q1[1], pick(q2[0], q2[1]), q3[1]])
        to_across = jnp.stack([own, pick(q1[1], q1[0]), q2[0], pick(q3[1], q3[0])])
        return [to_across, turn(to_sides, -1, 1), turn(to_across, 2, 1), turn(to_sides, 1, 1)]

    starts_at = [32 * at for at in starts]
    gathered_parts = [
        gathered(slice(at, at + 32 * n)) for at, n in zip(starts_at, PARTS)
    ]
    swap_lo = shift(jnp.where(keeper, w_lo, below), "c", 1)
    swap_hi = shift(jnp.where(keeper, w_hi, above), "c", 1)
    w_all = jnp.concatenate(
        [
            jnp.where(keeper, w_lo, swap_lo),
            jnp.where(keeper, w_hi, swap_hi),
            jnp.where(keeper, swap_lo, below),
            jnp.where(keeper, swap_hi, above),
        ],
        axis=0,
    )

    from_pair = jnp.where(low, p1[1024:], p3[1024:])
    from_pair = pick(from_pair, shift(from_pair, "c", 1))
    proj = (terms + from_pair.astype(jnp.float32)).astype(jnp.bfloat16)
    proj = jnp.concatenate([proj, proj], axis=0)
    proj_rows = jnp.concatenate(
        [proj, shift(proj[:, :256], "y", 1), shift(proj[:, 256:], "y", -1)], axis=1
    )

    columns = []
    for g in range(4):
        for u in range(4):
            options = []
            for x_off, z_off in ((u, g), (g, u)):
                far = (0, 1 - low.astype(jnp.int32), 1, low.astype(jnp.int32))[x_off]
                options.append(jnp.where(far == 0, xh, 1 - xh) * 4 + lax.rem(z + z_off, 4))
            columns.append(pick(*options))
    table = jnp.stack(columns + [1 - c, xl, 1 - xl])

    def finish(pieces, at, n):
        out = finish_part(table, pieces, w_all, bt[32 * at : 32 * (at + n)], proj_rows)
        got = lax.all_to_all(out.reshape(64, n, MESSAGE), PEERS, split_axis=0, concat_axis=0)
        got = got.astype(jnp.float32).reshape(2, 4, 8, n, MESSAGE).sum(axis=0)
        first = jnp.roll(got[..., 512:768], -1, axis=0)
        second = jnp.roll(got[..., 768:1024], 1, axis=0)
        kernel = got[..., :512] + jnp.concatenate([first, second], axis=-1)
        kernel = kernel.astype(jnp.bfloat16).transpose(2, 0, 1, 3).reshape(n, NAUX)
        return kernel, jnp.sum(got[..., 1024:1088] + got[..., 1088:], axis=(0, 1))

    parts = [finish(*part) for part in zip(gathered_parts, starts, PARTS)]
    kernel_rows = jnp.concatenate([k for k, _ in parts], axis=0)
    coupling = jnp.concatenate([v for _, v in parts], axis=0)

    rows_here = 16
    first_row = ((xl * 2 + c) * 32 + y * 8 + xh * 4 + z) * rows_here
    occ_index = slab_first[0] + first_row // NV
    positions = jnp.arange(eps_occ.shape[0], dtype=jnp.int32)
    occupied = jnp.sum(jnp.where(positions == occ_index, eps_occ, 0.0))
    virtual = lax.dynamic_slice_in_dim(eps_virt, first_row % NV, rows_here, 0)
    diagonal = (virtual - occupied)[:, None]
    sigma = diagonal * trials.astype(jnp.float32) + coupling * (1.0 / math.sqrt(NAUX * NT))
    return (kernel_rows, sigma)


def solution(mesh):
    fine = Mesh(mesh.devices.reshape(tuple(SIZES.values())), AXES)
    in_specs = (P(GRP, PANEL), P(GRP, PANEL), P(), P(PANEL + GRP, None), P(), P(), P())
    out_specs = (P(PANEL + GRP, None), P(PANEL + GRP, None))
    return jax.shard_map(
        on_device, mesh=fine, in_specs=in_specs, out_specs=out_specs, check_vma=False
    )
```
